256 devices in a mesh: zero: 2 (over z_hi), expert: 128 (over y, x, z_lo, core).
Axes of the slice: x: 4, y: 4, z: 8 (z_hi: 2, z_lo: 4; z = z_hi * 4 + z_lo), core: 2. Of those that a mesh axis runs over, the one named last changes fastest.
Arguments:
- tokens: bfloat16 [32768, 2048], P(('zero', 'expert')), may hold values from -6 to 6
- cotangent: bfloat16 [32768, 2048], P(('zero', 'expert')), may hold values from -6 to 6
- expert_ids: int32 [32768, 2], P(('zero', 'expert')), may hold values from 0 to 127, all different within a row; in each aligned block of 128 rows (0 to 127, 128 to 255, ...) at most 4 rows name the same one
- gate_values: float32 [32768, 2], P(('zero', 'expert')), may hold values from 0.1 to 1
- w_gate: bfloat16 [128, 768, 2048], P('expert', 'zero'), may hold values from -0.125 to 0.125
- w_up: bfloat16 [128, 768, 2048], P('expert', 'zero'), may hold values from -0.125 to 0.125
- w_down: bfloat16 [128, 768, 2048], P('expert', 'zero'), may hold values from -0.21875 to 0.21875
Outputs:
- layer_out: bfloat16 [32768, 2048], P(('zero', 'expert'))
- token_grad: bfloat16 [32768, 2048], P(('zero', 'expert'))
- grad_gate: bfloat16 [128, 768, 2048], P('expert', 'zero')
- grad_up: bfloat16 [128, 768, 2048], P('expert', 'zero')
- grad_down: bfloat16 [128, 768, 2048], P('expert', 'zero')
The draws below stay inside these ranges and needn't reach their ends.
Inputs may be any that keep to these rules, and one draw needn't show every extreme that they name: `expert_ids`: the 2 experts of a row differ. In each aligned block of 128 rows (the rows of one device) no expert is named more than 4 times, a bound that some block reaches.
All inputs are finite; a program needn't handle non-finite values.
Results may differ from the reference program's by a relative error of at most 0.0065.
Values may be sent and summed in bfloat16 or wider, within the bound.
A program may use at most 128 MiB of HBM per device.

```python
import math
import jax
import jax.numpy as jnp
import numpy as np
from jax import lax

D = 2048
FF = 768
EXPERTS = 128
TOP = 2
TOK_DEV = 128
CAP = 4
TOKENS = 32768
N_ZERO = 2
N_EXPERT = 128


def steps_of(own_key, extent, pieces, low, high):
    gain, own = 1.0, jax.random.fold_in(own_key, 6)
    for position, shards_of in pieces:
        heights = jnp.exp(jax.random.uniform(jax.random.fold_in(own, position), (shards_of,), jnp.float32, low / len(pieces), high / len(pieces)))
        gain = gain * jnp.repeat(heights, extent[position] // shards_of).reshape([-1 if axis == position else 1 for axis in range(len(extent))])
    return gain


def routed_block(own_key, own, number, rows, count, top, bound, slope):
    order = jax.random.permutation(own_key, count)
    crowded, usual = load_shares(count, rows * top, bound, slope, True), load_shares(count, rows * top, bound, slope, False)
    places = jnp.arange(count)

    def named(lengths, offset_by):
        used = int((lengths > 0).sum())
        fixed = max(1, used // 4)
        moved = fixed + (places - fixed + offset_by * (used - fixed)) % max(1, count - fixed)
        return jnp.zeros((count,), jnp.int32).at[order[jnp.where(places < fixed, places, moved)]].set(jnp.asarray(lengths, jnp.int32))

    lengths = jnp.where(number % 4 == 0, named(crowded, number // 4), named(usual, number - number // 4 - 1))
    mixed = jax.random.permutation(jax.random.fold_in(own, 3), count)
    giver, taker = mixed[0:count // 2 * 2:2], mixed[1:count // 2 * 2:2]
    room = jnp.minimum(lengths[giver] - 1, bound - lengths[taker]) // 2
    room = jnp.where((giver == order[0]) | (taker == order[0]) | (lengths[taker] == 0), 0, jnp.maximum(room, 0))
    moved = jax.random.randint(jax.random.fold_in(own, 4), (count // 2,), 0, 1 << 20) % (room + 1)
    lengths = lengths.at[giver].add(-moved).at[taker].add(moved)
    items = jnp.searchsorted(jnp.cumsum(lengths), jnp.arange(rows * top), side="right").astype(jnp.int32)
    listing = items.reshape(top, rows).T
    listing = listing[jax.random.permutation(jax.random.fold_in(own, 1), rows)]
    offset_by = jax.random.randint(jax.random.fold_in(own, 2), (rows, 1), 0, top)
    return jnp.take_along_axis(listing, (jnp.arange(top)[None, :] + offset_by) % top, axis=1)


def load_shares(number_of, total, most, lean, full):
    portions = [(1 << 20) // math.isqrt(rank ** lean) + 1 for rank in range(1, number_of + 1)]
    largest = most if full else min(most, max(-(-total // number_of), total * portions[0] // sum(portions)))
    least = 1 if total - largest >= number_of - 1 else 0
    holding, surplus = [largest] + [least] * (number_of - 1), total - largest - least * (number_of - 1)
    while surplus > 0:
        free = [i for i in range(1, number_of) if holding[i] < largest] or [i for i in range(1, number_of) if holding[i] < most]
        mass, budget = sum([portions[i] for i in free]), surplus
        for i in free:
            addition = min(most - holding[i], max(1, budget * portions[i] // mass), surplus)
            holding[i] = holding[i] + addition
            surplus = surplus - addition
    return np.array(holding)


def normal_values(rng, dims, spread, reach, split=(), kind=jnp.bfloat16):
    array = jax.random.normal(rng, dims, jnp.float32) * spread
    if len(split) > 0:
        array = steps_of(rng, dims, split, -0.22, 0.18) * array
    return jnp.clip(array, min=-reach, max=reach).astype(kind)


def setup_inputs(seed: int = 0) -> dict:
    key_list = jax.random.split(jax.random.key(seed), 8)
    tokens = normal_values(key_list[0], (TOKENS, D), 1.0, 6.0, ((0, 256),))
    cotangent = normal_values(key_list[1], (TOKENS, D), 1.0, 6.0, ((0, 256),))
    expert_ids_keys = jax.random.split(jax.random.fold_in(key_list[2], 1), TOKENS // TOK_DEV)
    expert_ids_turns = jax.random.permutation(jax.random.fold_in(key_list[2], 3), TOKENS // TOK_DEV)
    expert_ids = jax.vmap(lambda own, number: routed_block(jax.random.fold_in(key_list[2], 2), own, number, TOK_DEV, EXPERTS, TOP, CAP, 2))(expert_ids_keys, expert_ids_turns).reshape((TOKENS, TOP))
    gate_values = jnp.clip(0.1 + 0.9 * jax.random.uniform(key_list[3], (TOKENS, TOP), jnp.float32) ** steps_of(key_list[3], (TOKENS, TOP), ((0, 256),), -0.2, 0.2), 0.1, 1.0)
    w_gate = normal_values(key_list[4], (EXPERTS, FF, D), D ** -0.5, 0.125, ((0, 128), (1, 2)))
    w_up = normal_values(key_list[5], (EXPERTS, FF, D), D ** -0.5, 0.125, ((0, 128), (1, 2)))
    w_down = normal_values(key_list[6], (EXPERTS, FF, D), FF ** -0.5, 0.21875, ((0, 128), (1, 2)))
    return dict(tokens=tokens, cotangent=cotangent, expert_ids=expert_ids, gate_values=gate_values, w_gate=w_gate, w_up=w_up, w_down=w_down)


def swiglu_forward(row_data, weight_gate, weight_up):
    pre_gate = jnp.dot(row_data, weight_gate.T, preferred_element_type=jnp.float32)
    pre_up = jnp.dot(row_data, weight_up.T, preferred_element_type=jnp.float32)
    hidden = (jax.nn.silu(pre_gate) * pre_up).astype(jnp.bfloat16)
    return pre_gate, pre_up, hidden


def swiglu_backward(pre_gate, pre_up, cot_rows, weight_down):
    hidden_grad = jnp.dot(cot_rows, weight_down.T, preferred_element_type=jnp.float32)
    sigmoid = jax.nn.sigmoid(pre_gate)
    gate_grad = (hidden_grad * pre_up * (sigmoid * (1.0 + pre_gate * (1.0 - sigmoid)))).astype(jnp.bfloat16)
    up_grad = (hidden_grad * (pre_gate * sigmoid)).astype(jnp.bfloat16)
    return gate_grad, up_grad


def slot_table(expert_ids):
    blocks = expert_ids.reshape(N_ZERO * N_EXPERT, TOK_DEV * TOP).astype(jnp.int32)
    onehot = (blocks[:, :, None] == jnp.arange(EXPERTS, dtype=jnp.int32)[None, None, :]).astype(jnp.int32)
    earlier = (jnp.cumsum(onehot, axis=1) - onehot).astype(jnp.int32)
    ranking = jnp.sum(earlier * onehot, axis=2).astype(jnp.int32)
    block_index = jnp.arange(N_ZERO * N_EXPERT, dtype=jnp.int32)[:, None]
    row_in_expert = block_index * CAP + ranking
    token_index = block_index * TOK_DEV + jnp.arange(TOK_DEV * TOP, dtype=jnp.int32)[None, :] // TOP
    return blocks, row_in_expert, token_index


def reference(tokens, cotangent, expert_ids, gate_values, w_gate, w_up, w_down):
    blocks, row_in_expert, token_index = slot_table(expert_ids)
    total_rows = N_ZERO * N_EXPERT * CAP
    source = jnp.full((EXPERTS, total_rows), -1, jnp.int32)
    source = source.at[blocks.reshape(-1), row_in_expert.reshape(-1)].set(token_index.reshape(-1))
    gate_table = jnp.zeros((EXPERTS, total_rows), gate_values.dtype)
    gate_table = gate_table.at[blocks.reshape(-1), row_in_expert.reshape(-1)].set(gate_values.reshape(-1))

    def per_expert(carried, inputs):
        layer_acc, grad_acc = carried
        source_row, gate_row, weight_gate, weight_up, weight_down = inputs
        is_live = source_row >= 0
        gather_index = jnp.where(is_live, source_row, 0).astype(jnp.int32)
        row_data = jnp.where(is_live[:, None], tokens[gather_index], jnp.zeros((), tokens.dtype))
        cot_rows = (gate_row[:, None] * cotangent[gather_index].astype(jnp.float32)).astype(jnp.bfloat16)
        pre_gate, pre_up, hidden = swiglu_forward(row_data, weight_gate, weight_up)
        expert_out = jnp.dot(hidden, weight_down, preferred_element_type=jnp.float32).astype(jnp.bfloat16)
        gate_grad, up_grad = swiglu_backward(pre_gate, pre_up, cot_rows, weight_down)
        row_grad = (jnp.dot(gate_grad, weight_gate, preferred_element_type=jnp.float32)
                    + jnp.dot(up_grad, weight_up, preferred_element_type=jnp.float32)).astype(jnp.bfloat16)
        layer_acc = layer_acc.at[gather_index].add(gate_row[:, None] * expert_out.astype(jnp.float32))
        grad_acc = grad_acc.at[gather_index].add(jnp.where(is_live[:, None], row_grad.astype(jnp.float32), 0.0))
        gate_weight_grad = jnp.dot(gate_grad.T, row_data, preferred_element_type=jnp.float32).astype(jnp.bfloat16)
        up_weight_grad = jnp.dot(up_grad.T, row_data, preferred_element_type=jnp.float32).astype(jnp.bfloat16)
        down_weight_grad = jnp.dot(hidden.T, cot_rows, preferred_element_type=jnp.float32).astype(jnp.bfloat16)
        return (layer_acc, grad_acc), (gate_weight_grad, up_weight_grad, down_weight_grad)

    start_carry = (jnp.zeros((TOKENS, D), jnp.float32), jnp.zeros((TOKENS, D), jnp.float32))
    (layer_acc, grad_acc), (grad_gate, grad_up, grad_down) = lax.scan(
        per_expert, start_carry, (source, gate_table, w_gate, w_up, w_down))
    return (layer_acc.astype(jnp.bfloat16), grad_acc.astype(jnp.bfloat16), grad_gate, grad_up, grad_down)
```

```python
import functools

import jax
import jax.numpy as jnp
from jax import lax
from jax.experimental import pallas as pl
from jax.experimental.pallas import tpu as pltpu
from jax.sharding import PartitionSpec as P

MESH = pl.DeviceIdType.MESH
BF16, F32, I32 = jnp.bfloat16, jnp.float32, jnp.int32

RING = 8
PLANE = 32
WIDE = 256
CAP = 4
SOURCE_ROWS = RING * CAP
FROM_LEFT = {0: 0, 1: 1, 2: 3, 3: 5, 4: 7}
FROM_RIGHT = {0: 0, 1: 2, 2: 4, 3: 6, 4: 7}


def dot(a, b):
    return lax.dot_general(a, b, (((1,), (0,)), ((), ())), preferred_element_type=F32)


def dot_nt(a, b):
    return lax.dot_general(a, b, (((1,), (1,)), ((), ())), preferred_element_type=F32)


def kernel(
    ids_c, ids_r, gate_r, tok, cot, wg, wu, wd,
    layer_out, token_grad, grad_gate, grad_up, grad_down,
    G, S, X, Q, RS, WB, F, H, T, D, C, GR, M,
    load_sem, wload_sem, meta_send, meta_recv, ring_send, ring_recv,
    out_send, out_recv, back_send, back_recv, rs_send, rs_recv, store_sem, wstore_sem,
):
    n = G.shape[0]
    tok_rows = G.shape[3]
    expert = lax.axis_index("expert")
    core = expert % 2
    z_lo = (expert // 2) % 4
    x = (expert // 8) % 4
    y = expert // 32
    z = lax.axis_index("zero") * 4 + z_lo

    def along_z(step):
        to = (z + step + RING) % RING
        return (to // 4, ((y * 4 + x) * 4 + to % 4) * 2 + core)

    def in_plane(j, sign):
        to_y = (y + sign * (j // 8) + 4) % 4
        to_x = (x + sign * ((j // 2) % 4) + 4) % 4
        to_c = (core + j % 2) % 2
        return (z // 4, ((to_y * 4 + to_x) * 4 + z_lo) * 2 + to_c)

    def columns(c):
        return pl.ds(pl.multiple_of(c * WIDE, WIDE), WIDE)

    def loads(c):
        return [
            pltpu.make_async_copy(ref.at[:, columns(c)], G.at[c, 0, a], load_sem.at[c, a])
            for a, ref in enumerate((tok, cot))
        ]

    def start_load(c, carry):
        for copy in loads(c):
            copy.start()
        return carry

    lax.fori_loop(0, n, start_load, 0)

    barrier = pltpu.get_barrier_semaphore()

    def greet(j, carry):
        pl.semaphore_signal(barrier, inc=1, device_id=in_plane(j, 1), device_id_type=MESH)
        return carry

    lax.fori_loop(1, PLANE, greet, 0)
    for step in range(1, RING):
        pl.semaphore_signal(barrier, inc=1, device_id=along_z(step), device_id_type=MESH)

    def start_weights(c, carry):
        for i, ref in enumerate((wg, wu, wd)):
            pltpu.make_async_copy(ref.at[0, :, columns(c)], WB.at[i, c], wload_sem).start()
        return carry

    lax.fori_loop(0, n, start_weights, 0)

    earlier = lax.broadcasted_iota(I32, (tok_rows, tok_rows), 0) < lax.broadcasted_iota(
        I32, (tok_rows, tok_rows), 1
    )
    for k in range(2):
        same = jnp.zeros((tok_rows, tok_rows), F32)
        for k2 in range(2):
            same += jnp.where((ids_c[:, k2 : k2 + 1] == ids_r[k : k + 1, :]) & earlier, 1.0, 0.0)
        slot = jnp.sum(same, axis=0, keepdims=True)
        M[0, k : k + 1, :] = ids_r[k : k + 1, :].astype(F32) * CAP + slot
    M[0, 2:4, :] = gate_r[...]
    M[0, 4:8, :] = jnp.zeros((4, tok_rows), F32)

    pl.semaphore_wait(barrier, PLANE - 1 + RING - 1)

    def remote(src, dst, send, recv, to):
        return pltpu.make_async_remote_copy(
            src_ref=src, dst_ref=dst, send_sem=send, recv_sem=recv, device_id=to, device_id_type=MESH
        )

    right, left = along_z(1), along_z(-1)

    def ring_copies(c, hop):
        got_l, got_r = FROM_LEFT[hop - 1], FROM_RIGHT[hop - 1]
        to_l, to_r = FROM_LEFT[hop], FROM_RIGHT[hop]
        if hop < 4:
            return (
                remote(G.at[c, got_l], G.at[c, to_l], ring_send.at[c, 2 * hop - 2], ring_recv.at[c, to_l], right),
                remote(G.at[c, got_r], G.at[c, to_r], ring_send.at[c, 2 * hop - 1], ring_recv.at[c, to_r], left),
            )
        return (
            remote(G.at[c, got_l, 0], G.at[c, 7, 0], ring_send.at[c, 6], ring_recv.at[c, 7], right),
            remote(G.at[c, got_r, 1], G.at[c, 7, 1], ring_send.at[c, 7], ring_recv.at[c, 0], left),
        )

    def ring_hop(c, hop):
        if hop == 1:
            for copy in loads(c):
                copy.wait()
            for copy in ring_copies(c, 1):
                copy.start()
        else:
            for before, copy in zip(ring_copies(c, hop - 1), ring_copies(c, hop)):
                before.wait_recv()
                copy.start()

    def ring_end(c):
        for copy in ring_copies(c, 4):
            copy.wait_recv()

    ring_hop(0, 1)
    metas = []
    for slot, step in enumerate((0, 1, -1, 2, -2, 3, -3, 4)):
        if step:
            metas.append(remote(M.at[0], M.at[slot], meta_send.at[slot], meta_recv.at[slot], along_z(step)))
    for copy in metas:
        copy.start()
    ring_hop(1, 1)
    ring_hop(0, 2)
    F[...] = jnp.zeros(F.shape, F32)
    for copy in metas:
        copy.wait_recv()
    ring_hop(0, 3)

    def place(position, i):
        e = position.astype(I32) // CAP
        s = position.astype(I32) % CAP
        mine = ((e // 2) % 4) == z_lo
        j = ((e // 32 - y + 4) % 4) * 8 + ((e // 8 - x + 4) % 4) * 2 + (e - core + 2) % 2
        return jnp.where(mine, j * 16 + i * CAP + s, -1)

    half = PLANE * 16
    row_id = lax.broadcasted_iota(I32, (half, tok_rows), 0)
    col_id = lax.broadcasted_iota(I32, (tok_rows, half), 1)
    for g in range(2):
        gates = jnp.zeros((half, tok_rows), F32)
        for i in range(4):
            m = M[4 * g + i]
            mt = jnp.transpose(m)
            tokens_i = slice(i * tok_rows, (i + 1) * tok_rows)
            first, second = row_id == place(m[0:1], i), row_id == place(m[1:2], i)
            D[g, :, tokens_i] = jnp.where(first | second, 1.0, 0.0).astype(BF16)
            gates += jnp.where(first, m[2:3], 0.0) + jnp.where(second, m[3:4], 0.0)
            first, second = col_id == place(mt[:, 0:1], i), col_id == place(mt[:, 1:2], i)
            C[0, g, tokens_i, :] = jnp.where(first | second, 1.0, 0.0).astype(BF16)
            weight = jnp.where(first, mt[:, 2:3], 0.0) + jnp.where(second, mt[:, 3:4], 0.0)
            high = weight.astype(BF16)
            C[1, g, tokens_i, :] = high
            C[2, g, tokens_i, :] = (weight - high.astype(F32)).astype(BF16)
        GR[g] = jnp.broadcast_to(jnp.sum(gates, axis=1, keepdims=True), (half, 128))
    ring_hop(0, 4)

    def pick(c):
        for g in range(2):
            rows = slice(16 * g, 16 * g + 16)
            for a in range(2):
                block = G[c, 4 * g : 4 * g + 4, a].reshape(4 * tok_rows, WIDE)
                picked = dot(D[g], block)
                if a == 1:
                    picked = picked * jnp.concatenate([GR[g]] * (WIDE // 128), axis=1)
                S[c, :, a, rows, :] = picked.astype(BF16).reshape(PLANE, 16, WIDE)
        X[c, 0] = S[c, 0]

    def send(c, dst, sign, send_sem, recv_sem):
        def one(j, carry):
            remote(S.at[c, j], dst.at[c, j], send_sem.at[c], recv_sem.at[c], in_plane(j, sign)).start()
            return carry

        lax.fori_loop(1, PLANE, one, 0)

    def all_of(c, dst, send_sem, recv_sem):
        others = pl.ds(1, PLANE - 1)
        return remote(S.at[c, others], dst.at[c, others], send_sem.at[c], recv_sem.at[c], right)

    def row_tile(c, a, m):
        return X[c, pl.ds(8 * m, 8), a].reshape(8 * SOURCE_ROWS, WIDE)

    def tile_rows(m):
        return pl.ds(pl.multiple_of(m * 256, 256), 256)

    def unit_cols(i):
        units = WB.shape[2]
        return slice(i * units, (i + 1) * units)

    def before_act(c):
        all_of(c, X, out_send, out_recv).wait_recv()

        def tile(m, carry):
            rows, cots = row_tile(c, 0, m), row_tile(c, 1, m)
            for i, block in enumerate((rows, rows, cots)):
                F[tile_rows(m), unit_cols(i)] += dot_nt(block, WB[i, c])
            return carry

        lax.fori_loop(0, 4, tile, 0)

    pltpu.make_async_copy(WB, WB, wload_sem).wait()

    def way_out(t, carry):
        @pl.when(t + 2 < n)
        def _():
            ring_hop(t + 2, 1)

        @pl.when(t + 1 < n)
        def _():
            ring_hop(t + 1, 2)

        ring_end(t)
        pick(t)
        send(t, X, 1, out_send, out_recv)

        @pl.when(t + 1 < n)
        def _():
            ring_hop(t + 1, 3)

        @pl.when(t >= 2)
        def _():
            before_act(t - 2)

        @pl.when(t + 1 < n)
        def _():
            ring_hop(t + 1, 4)

        return carry

    lax.fori_loop(0, n, way_out, 0)
    before_act(n - 2)
    before_act(n - 1)

    def activate(m, carry):
        pre_gate, pre_up, hidden_grad = (F[tile_rows(m), unit_cols(i)] for i in range(3))
        sigmoid = jax.nn.sigmoid(pre_gate)
        silu = pre_gate * sigmoid
        hidden = silu * pre_up
        gate_grad = hidden_grad * pre_up * (sigmoid * (1.0 + pre_gate * (1.0 - sigmoid)))
        up_grad = hidden_grad * silu
        for i, v in enumerate((gate_grad, up_grad, hidden)):
            H[i, m] = v.astype(BF16)
            T[i, m] = jnp.transpose(v).astype(BF16)
        return carry

    lax.fori_loop(0, 4, activate, 0)

    def answer(c, carry):
        all_of(c, X, out_send, out_recv).wait_send()

        def tile(m, carry):
            expert_out = dot(H[2, m], WB[2, c])
            row_grad = dot(H[0, m], WB[0, c]) + dot(H[1, m], WB[1, c])
            S[c, pl.ds(8 * m, 8), 0] = expert_out.astype(BF16).reshape(8, SOURCE_ROWS, WIDE)
            S[c, pl.ds(8 * m, 8), 1] = row_grad.astype(BF16).reshape(8, SOURCE_ROWS, WIDE)
            return carry

        lax.fori_loop(0, 4, tile, 0)
        Q[c, 0] = S[c, 0]
        send(c, Q, -1, back_send, back_recv)
        return carry

    lax.fori_loop(0, n, answer, 0)

    def ring_sent(c, carry):
        for hop in range(1, 5):
            for copy in ring_copies(c, hop):
                copy.wait_send()
        return carry

    lax.fori_loop(0, n, ring_sent, 0)

    def part_cols(c, a):
        return columns((c % 2) * 2 + a)

    def combine(c):
        all_of(c, Q, back_send, back_recv).wait_recv()
        for g in range(2):
            rows = slice(16 * g, 16 * g + 16)
            frames = slice(4 * tok_rows * g, 4 * tok_rows * (g + 1))
            outs = Q[c, :, 0, rows, :].reshape(half, WIDE)
            F[frames, part_cols(c, 0)] = dot(C[1, g], outs) + dot(C[2, g], outs)
            grads = Q[c, :, 1, rows, :].reshape(half, WIDE)
            F[frames, part_cols(c, 1)] = dot(C[0, g], grads)

    def part(c, slot, a):
        return F[slot * tok_rows : (slot + 1) * tok_rows, part_cols(c, a)]

    def rs_copies(c, hop):
        if hop == 1:
            return (
                remote(G.at[c, 7, 0], RS.at[c, 0, 3, 0], rs_send.at[c, 0, 3], rs_recv.at[c, 0, 3], right),
                remote(G.at[c, 7, 1], RS.at[c, 1, 3, 1], rs_send.at[c, 1, 3], rs_recv.at[c, 1, 3], left),
            )
        at, to = 5 - hop, 4 - hop
        return tuple(
            remote(RS.at[c, way, at], RS.at[c, way, to], rs_send.at[c, way, to], rs_recv.at[c, way, to], whom)
            for way, whom in enumerate((right, left))
        )

    def rs_hop(c, hop):
        copies = rs_copies(c, hop)
        if hop == 1:
            for a in range(2):
                G[c, 7, a] = part(c, 7, a).astype(BF16)
                copies[a].start()
            return
        at = 5 - hop
        for way, slots in enumerate((FROM_RIGHT, FROM_LEFT)):
            rs_copies(c, hop - 1)[way].wait_recv()
            for a in range(2):
                total = part(c, slots[at], a)
                if hop > 2 or a == way:
                    total = total + RS[c, way, at, a].astype(F32)
                RS[c, way, at, a] = total.astype(BF16)
            copies[way].start()

    def stores(c):
        return [
            pltpu.make_async_copy(G.at[c, 0, a], ref.at[:, columns(c)], store_sem.at[c, a])
            for a, ref in enumerate((layer_out, token_grad))
        ]

    def rs_end(c):
        for copy in rs_copies(c, 4):
            copy.wait_recv()
        for a, copy in enumerate(stores(c)):
            total = part(c, 0, a) + RS[c, 0, 0, a].astype(F32) + RS[c, 1, 0, a].astype(F32)
            G[c, 0, a] = total.astype(BF16)
            copy.start()

    def wstore(c, i):
        ref = (grad_gate, grad_up, grad_down)[i]
        return pltpu.make_async_copy(WB.at[i, c], ref.at[0, :, columns(c)], wstore_sem.at[c, i])

    def weight_grad(c, i):
        a = 1 if i == 2 else 0
        total = dot(T[i, 0], row_tile(c, a, 0))
        for m in range(1, 4):
            total += dot(T[i, m], row_tile(c, a, m))
        WB[i, c] = total.astype(BF16)
        wstore(c, i).start()

    def way_back(c, carry):
        combine(c)
        rs_hop(c, 1)

        @pl.when(c >= 1)
        def _():
            rs_hop(c - 1, 3)

        weight_grad(c, 0)
        rs_hop(c, 2)
        weight_grad(c, 1)

        @pl.when(c >= 1)
        def _():
            rs_hop(c - 1, 4)

        weight_grad(c, 2)

        @pl.when(c >= 1)
        def _():
            rs_end(c - 1)

        return carry

    lax.fori_loop(0, n, way_back, 0)
    rs_hop(n - 1, 3)
    rs_hop(n - 1, 4)
    rs_end(n - 1)

    def finish(c, carry):
        for copy in stores(c):
            copy.wait()
        for i in range(3):
            wstore(c, i).wait()
        all_of(c, Q, back_send, back_recv).wait_send()
        for hop in range(1, 5):
            for copy in rs_copies(c, hop):
                copy.wait_send()
        return carry

    lax.fori_loop(0, n, finish, 0)
    for copy in metas:
        copy.wait_send()


def local(tokens, cotangent, expert_ids, gate_values, w_gate, w_up, w_down):
    tok_rows, width = tokens.shape
    hidden = w_gate.shape[1]
    n = width // WIDE
    rows = PLANE * SOURCE_ROWS
    half = PLANE * 16
    sem = pltpu.SemaphoreType.DMA
    vmem, hbm = pl.BlockSpec(memory_space=pltpu.VMEM), pl.BlockSpec(memory_space=pl.ANY)
    return pl.pallas_call(
        kernel,
        out_shape=[jax.ShapeDtypeStruct(v.shape, BF16) for v in (tokens, cotangent, w_gate, w_up, w_down)],
        in_specs=[vmem] * 3 + [hbm] * 5,
        out_specs=[hbm] * 5,
        scratch_shapes=[
            pltpu.VMEM((n, RING, 2, tok_rows, WIDE), BF16),
            pltpu.VMEM((n, PLANE, 2, SOURCE_ROWS, WIDE), BF16),
            pltpu.VMEM((n, PLANE, 2, SOURCE_ROWS, WIDE), BF16),
            pltpu.VMEM((n, PLANE, 2, SOURCE_ROWS, WIDE), BF16),
            pltpu.VMEM((n, 2, 4, 2, tok_rows, WIDE), BF16),
            pltpu.VMEM((3, n, hidden, WIDE), BF16),
            pltpu.VMEM((rows, max(3 * hidden, 4 * WIDE)), F32),
            pltpu.VMEM((3, 4, rows // 4, hidden), BF16),
            pltpu.VMEM((3, 4, hidden, rows // 4), BF16),
            pltpu.VMEM((2, half, 4 * tok_rows), BF16),
            pltpu.VMEM((3, 2, 4 * tok_rows, half), BF16),
            pltpu.VMEM((2, half, 128), F32),
            pltpu.VMEM((RING, 8, tok_rows), F32),
            sem((n, 2)), sem, sem((RING,)), sem((RING,)), sem((n, 8)), sem((n, 8)),
            sem((n,)), sem((n,)), sem((n,)), sem((n,)), sem((n, 2, 4)), sem((n, 2, 4)), sem((n, 2)), sem((n, 3)),
        ],
        compiler_params=pltpu.CompilerParams(
            collective_id=0, has_side_effects=True, vmem_limit_bytes=63 * 2**20
        ),
    )(expert_ids, expert_ids.T, gate_values.T, tokens, cotangent, w_gate, w_up, w_down)


def solution(mesh):
    rows = P(("zero", "expert"), None)
    weights = P("expert", "zero", None)
    return jax.shard_map(
        local,
        mesh=mesh,
        in_specs=(rows, rows, rows, rows, weights, weights, weights),
        out_specs=(rows, rows, weights, weights, weights),
        check_vma=False,
    )
```

```python
import functools

import jax
import jax.numpy as jnp
from jax import lax
from jax.experimental import pallas as pl
from jax.experimental.pallas import tpu as pltpu
from jax.sharding import PartitionSpec as P

MESH = pl.DeviceIdType.MESH
BF16, F32, I32 = jnp.bfloat16, jnp.float32, jnp.int32

RING = 8
PLANE = 32
WIDE = 256
CAP = 4
SOURCE_ROWS = RING * CAP
FROM_LEFT = {0: 0, 1: 1, 2: 3, 3: 5, 4: 7}
FROM_RIGHT = {0: 0, 1: 2, 2: 4, 3: 6, 4: 7}


def dot(a, b):
    return lax.dot_general(a, b, (((1,), (0,)), ((), ())), preferred_element_type=F32)


def dot_nt(a, b):
    return lax.dot_general(a, b, (((1,), (1,)), ((), ())), preferred_element_type=F32)


def kernel(
    ids_r, gate_r, tok, cot, wg, wu, wd,
    layer_out, token_grad, grad_gate, grad_up, grad_down,
    G, S, X, Q, RS, WB, F, H, T, D, C, GR, M,
    load_sem, wload_sem, meta_send, meta_recv, ring_send, ring_recv,
    out_send, out_recv, back_send, back_recv, rs_send, rs_recv, store_sem, wstore_sem,
):
    n = G.shape[0]
    tok_rows = G.shape[3]
    expert = lax.axis_index("expert")
    core = expert % 2
    z_lo = (expert // 2) % 4
    x = (expert // 8) % 4
    y = expert // 32
    z = lax.axis_index("zero") * 4 + z_lo

    def along_z(step):
        to = (z + step + RING) % RING
        return (to // 4, ((y * 4 + x) * 4 + to % 4) * 2 + core)

    def in_plane(j, sign):
        to_y = (y + sign * (j // 8) + 4) % 4
        to_x = (x + sign * ((j // 2) % 4) + 4) % 4
        to_c = (core + j % 2) % 2
        return (z // 4, ((to_y * 4 + to_x) * 4 + z_lo) * 2 + to_c)

    def columns(c):
        return pl.ds(pl.multiple_of(c * WIDE, WIDE), WIDE)

    def loads(c):
        return [
            pltpu.make_async_copy(ref.at[:, columns(c)], G.at[c, 0, a], load_sem.at[c, a])
            for a, ref in enumerate((tok, cot))
        ]

    def start_load(c, carry):
        for copy in loads(c):
            copy.start()
        return carry

    lax.fori_loop(0, n, start_load, 0)

    barrier = pltpu.get_barrier_semaphore()

    def greet(j, carry):
        pl.semaphore_signal(barrier, inc=1, device_id=in_plane(j, 1), device_id_type=MESH)
        return carry

    lax.fori_loop(1, PLANE, greet, 0)
    for step in range(1, RING):
        pl.semaphore_signal(barrier, inc=1, device_id=along_z(step), device_id_type=MESH)

    def start_weights(c, carry):
        for i, ref in enumerate((wg, wu, wd)):
            pltpu.make_async_copy(ref.at[0, :, columns(c)], WB.at[i, c], wload_sem).start()
        return carry

    lax.fori_loop(0, n, start_weights, 0)

    earlier = lax.broadcasted_iota(I32, (tok_rows, tok_rows), 0) < lax.broadcasted_iota(
        I32, (tok_rows, tok_rows), 1
    )
    M[0] = jnp.zeros((8, tok_rows), F32)
    M[0, 0:2, :] = ids_r[...].astype(F32)
    ids_c = jnp.transpose(M[0])
    for k in range(2):
        own = ids_r[k : k + 1, :].astype(F32)
        same = jnp.zeros((tok_rows, tok_rows), F32)
        for k2 in range(2):
            same += jnp.where((ids_c[:, k2 : k2 + 1] == own) & earlier, 1.0, 0.0)
        slot = jnp.sum(same, axis=0, keepdims=True)
        M[0, k : k + 1, :] = own * CAP + slot
    M[0, 2:4, :] = gate_r[...]

    pl.semaphore_wait(barrier, PLANE - 1 + RING - 1)

    def remote(src, dst, send, recv, to):
        return pltpu.make_async_remote_copy(
            src_ref=src, dst_ref=dst, send_sem=send, recv_sem=recv, device_id=to, device_id_type=MESH
        )

    right, left = along_z(1), along_z(-1)

    def ring_copies(c, hop, a):
        got_l, got_r = FROM_LEFT[hop - 1], FROM_RIGHT[hop - 1]
        to_l, to_r = FROM_LEFT[hop], FROM_RIGHT[hop]
        ways = (
            (got_l, to_l, 2 * hop - 2, right),
            (got_r, to_r, 2 * hop - 1, left),
        )
        if hop == 4:
            ways = ways[a : a + 1]
        return [
            remote(G.at[c, got, a], G.at[c, to, a], ring_send.at[c, number, a], ring_recv.at[c, to, a], whom)
            for got, to, number, whom in ways
        ]

    def ring_hop(c, hop):
        for a in range(2):
            if hop == 1:
                loads(c)[a].wait()
            else:
                for copy in came_in(c, hop - 1, a, hop == 4):
                    copy.wait_recv()
            for copy in ring_copies(c, hop, a):
                copy.start()

    def came_in(c, hop, a, forwarded=False):
        copies = ring_copies(c, hop, a)
        return copies[a : a + 1] if forwarded else copies

    def ring_end(c):
        for a in range(2):
            ring_copies(c, 3, a)[1 - a].wait_recv()
        for a in range(2):
            ring_copies(c, 4, a)[0].wait_recv()

    ring_hop(0, 1)
    metas = []
    for slot, step in enumerate((0, 1, -1, 2, -2, 3, -3, 4)):
        if step:
            metas.append(remote(M.at[0], M.at[slot], meta_send.at[slot], meta_recv.at[slot], along_z(step)))
    for copy in metas:
        copy.start()
    ring_hop(0, 2)
    for copy in metas:
        copy.wait_recv()

    def place(position, i):
        e = position.astype(I32) // CAP
        s = position.astype(I32) % CAP
        mine = ((e // 2) % 4) == z_lo
        j = ((e // 32 - y + 4) % 4) * 8 + ((e // 8 - x + 4) % 4) * 2 + (e - core + 2) % 2
        return jnp.where(mine, j * 16 + i * CAP + s, -1)

    half = PLANE * 16

    def build_pick(g):
        row_id = lax.broadcasted_iota(I32, (half, tok_rows), 0)
        gates = jnp.zeros((half, tok_rows), F32)
        for i in range(4):
            m = M[4 * g + i]
            first, second = row_id == place(m[0:1], i), row_id == place(m[1:2], i)
            D[g, :, i * tok_rows : (i + 1) * tok_rows] = jnp.where(first | second, 1.0, 0.0).astype(BF16)
            gates += jnp.where(first, m[2:3], 0.0) + jnp.where(second, m[3:4], 0.0)
        GR[g] = jnp.broadcast_to(jnp.sum(gates, axis=1, keepdims=True), (half, 128))

    def build_put(g):
        col_id = lax.broadcasted_iota(I32, (tok_rows, half), 1)
        for i in range(4):
            mt = jnp.transpose(M[4 * g + i])
            tokens_i = slice(i * tok_rows, (i + 1) * tok_rows)
            first, second = col_id == place(mt[:, 0:1], i), col_id == place(mt[:, 1:2], i)
            C[0, g, tokens_i, :] = jnp.where(first | second, 1.0, 0.0).astype(BF16)
            weight = jnp.where(first, mt[:, 2:3], 0.0) + jnp.where(second, mt[:, 3:4], 0.0)
            high = weight.astype(BF16)
            C[1, g, tokens_i, :] = high
            C[2, g, tokens_i, :] = (weight - high.astype(F32)).astype(BF16)

    def group(g):
        return slice(16 * g, 16 * g + 16)

    def pick(c, g):
        for a in range(2):
            block = G[c, 4 * g : 4 * g + 4, a].reshape(4 * tok_rows, WIDE)
            picked = dot(D[g], block)
            if a == 1:
                picked = picked * jnp.concatenate([GR[g]] * (WIDE // 128), axis=1)
            S[c, :, a, group(g), :] = picked.astype(BF16).reshape(PLANE, 16, WIDE)
        X[c, 0, :, group(g), :] = S[c, 0, :, group(g), :]

    def send(c, dst, sign, send_sem, recv_sem, g=None):
        rows = slice(0, SOURCE_ROWS) if g is None else group(g)

        def one(j, carry):
            remote(S.at[c, j, :, rows], dst.at[c, j, :, rows], send_sem, recv_sem, in_plane(j, sign)).start()
            return carry

        lax.fori_loop(1, PLANE, one, 0)

    def all_of(c, dst, send_sem, recv_sem, g=None):
        others, rows = pl.ds(1, PLANE - 1), slice(0, SOURCE_ROWS) if g is None else group(g)
        return remote(S.at[c, others, :, rows], dst.at[c, others, :, rows], send_sem, recv_sem, right)

    def all_out(c):
        return all_of(c, X, out_send.at[c], out_recv.at[c])

    def row_tile(c, a, m):
        return X[c, pl.ds(8 * m, 8), a].reshape(8 * SOURCE_ROWS, WIDE)

    def tile_rows(m):
        return pl.ds(pl.multiple_of(m * 256, 256), 256)

    def unit_cols(i):
        units = WB.shape[2]
        return slice(i * units, (i + 1) * units)

    def before_act(c):
        all_out(c).wait_recv()

        def tile(m, carry):
            rows, cots = row_tile(c, 0, m), row_tile(c, 1, m)
            for i, block in enumerate((rows, rows, cots)):
                F[tile_rows(m), unit_cols(i)] += dot_nt(block, WB[i, c])
            return carry

        lax.fori_loop(0, 4, tile, 0)

    def send_out(c, g=None):
        send(c, X, 1, out_send.at[c], out_recv.at[c], g)

    build_pick(0)
    ring_hop(0, 3)
    ring_hop(1, 1)
    pick(0, 0)
    send_out(0, 0)
    build_pick(1)
    ring_hop(0, 4)
    ring_hop(1, 2)
    F[...] = jnp.zeros(F.shape, F32)
    ring_hop(2, 1)
    ring_end(0)
    pick(0, 1)
    send_out(0, 1)
    ring_hop(1, 3)
    ring_hop(1, 4)
    pltpu.make_async_copy(WB, WB, wload_sem).wait()

    def way_out(t, carry):
        @pl.when(t + 2 < n)
        def _():
            ring_hop(t + 2, 1)

        @pl.when(t + 1 < n)
        def _():
            ring_hop(t + 1, 2)

        ring_end(t)
        pick(t, 0)
        pick(t, 1)
        send_out(t)

        @pl.when(t + 1 < n)
        def _():
            ring_hop(t + 1, 3)

        @pl.when(t >= 2)
        def _():
            before_act(t - 2)

        @pl.when(t + 1 < n)
        def _():
            ring_hop(t + 1, 4)

        return carry

    lax.fori_loop(1, n, way_out, 0)
    build_put(0)
    build_put(1)
    before_act(n - 2)
    before_act(n - 1)

    def activate(m, carry):
        pre_gate, pre_up, hidden_grad = (F[tile_rows(m), unit_cols(i)] for i in range(3))
        sigmoid = jax.nn.sigmoid(pre_gate)
        silu = pre_gate * sigmoid
        hidden = silu * pre_up
        gate_grad = hidden_grad * pre_up * (sigmoid * (1.0 + pre_gate * (1.0 - sigmoid)))
        up_grad = hidden_grad * silu
        for i, v in enumerate((gate_grad, up_grad, hidden)):
            H[i, m] = v.astype(BF16)
            T[i, m] = jnp.transpose(v).astype(BF16)
        return carry

    lax.fori_loop(0, 4, activate, 0)

    def answer(c, carry):
        all_out(c).wait_send()

        def tile(m, carry):
            expert_out = dot(H[2, m], WB[2, c])
            row_grad = dot(H[0, m], WB[0, c]) + dot(H[1, m], WB[1, c])
            S[c, pl.ds(8 * m, 8), 0] = expert_out.astype(BF16).reshape(8, SOURCE_ROWS, WIDE)
            S[c, pl.ds(8 * m, 8), 1] = row_grad.astype(BF16).reshape(8, SOURCE_ROWS, WIDE)
            return carry

        lax.fori_loop(0, 4, tile, 0)
        Q[c, 0] = S[c, 0]

        @pl.when(c < n - 1)
        def _():
            send(c, Q, -1, back_send.at[c], back_recv.at[c])

        return carry

    lax.fori_loop(0, n, answer, 0)
    for g in (1, 0):
        send(n - 1, Q, -1, back_send.at[n - 1 + g], back_recv.at[n - 1 + g], g)

    def ring_sent(c, carry):
        for hop in range(1, 5):
            for a in range(2):
                for copy in ring_copies(c, hop, a):
                    copy.wait_send()
        return carry

    lax.fori_loop(0, n, ring_sent, 0)

    def part(c, slot, a):
        g, frames = slot // 4, slice((slot % 4) * tok_rows, (slot % 4 + 1) * tok_rows)
        rows = Q[c, :, a, group(g), :].reshape(half, WIDE)
        if a == 0:
            return dot(C[1, g, frames, :], rows) + dot(C[2, g, frames, :], rows)
        return dot(C[0, g, frames, :], rows)

    def rs_copies(c, hop, a):
        if hop == 1:
            return [remote(G.at[c, 7, a], RS.at[c, a, 3, a], rs_send.at[c, a, 3, a], rs_recv.at[c, a, 3, a], (right, left)[a])]
        at, to = 5 - hop, 4 - hop
        return [
            remote(RS.at[c, way, at, a], RS.at[c, way, to, a], rs_send.at[c, way, to, a], rs_recv.at[c, way, to, a], whom)
            for way, whom in enumerate((right, left))
        ]

    def rs_hop(c, hop):
        for a in range(2):
            copies = rs_copies(c, hop, a)
            if hop == 1:
                G[c, 7, a] = part(c, 7, a).astype(BF16)
                copies[0].start()
                continue
            at = 5 - hop
            for way, slots in enumerate((FROM_RIGHT, FROM_LEFT)):
                total = part(c, slots[at], a)
                if hop > 2:
                    rs_copies(c, hop - 1, a)[way].wait_recv()
                elif a == way:
                    rs_copies(c, 1, a)[0].wait_recv()
                if hop > 2 or a == way:
                    total = total + RS[c, way, at, a].astype(F32)
                RS[c, way, at, a] = total.astype(BF16)
                copies[way].start()

    def stores(c):
        return [
            pltpu.make_async_copy(G.at[c, 0, a], ref.at[:, columns(c)], store_sem.at[c, a])
            for a, ref in enumerate((layer_out, token_grad))
        ]

    def rs_end(c):
        for a, copy in enumerate(stores(c)):
            total = part(c, 0, a)
            for way in range(2):
                rs_copies(c, 4, a)[way].wait_recv()
                total = total + RS[c, way, 0, a].astype(F32)
            G[c, 0, a] = total.astype(BF16)
            copy.start()

    def wstore(c, i):
        ref = (grad_gate, grad_up, grad_down)[i]
        return pltpu.make_async_copy(WB.at[i, c], ref.at[0, :, columns(c)], wstore_sem.at[c, i])

    def weight_grad(c, i):
        a = 1 if i == 2 else 0
        total = dot(T[i, 0], row_tile(c, a, 0))
        for m in range(1, 4):
            total += dot(T[i, m], row_tile(c, a, m))
        WB[i, c] = total.astype(BF16)
        wstore(c, i).start()

    def all_back(c, number, g=None):
        return all_of(c, Q, back_send.at[number], back_recv.at[number], g)

    def way_back(c, carry):
        all_back(c, c).wait_recv()
        rs_hop(c, 1)

        @pl.when(c >= 1)
        def _():
            rs_hop(c - 1, 3)

        @pl.when(c >= 2)
        def _():
            rs_end(c - 2)

        for i in range(3):
            weight_grad(c, i)
        rs_hop(c, 2)

        @pl.when(c >= 1)
        def _():
            rs_hop(c - 1, 4)

        return carry

    lax.fori_loop(0, n - 1, way_back, 0)
    rs_hop(n - 2, 3)
    rs_end(n - 3)
    for i in range(3):
        weight_grad(n - 1, i)
    rs_hop(n - 2, 4)
    all_back(n - 1, n, 1).wait_recv()
    rs_hop(n - 1, 1)
    rs_hop(n - 1, 2)
    rs_end(n - 2)
    all_back(n - 1, n - 1, 0).wait_recv()
    rs_hop(n - 1, 3)
    rs_hop(n - 1, 4)
    rs_end(n - 1)

    def finish(c, carry):
        for copy in stores(c):
            copy.wait()
        for i in range(3):
            wstore(c, i).wait()
        for hop in range(1, 5):
            for a in range(2):
                for copy in rs_copies(c, hop, a):
                    copy.wait_send()

        @pl.when(c < n - 1)
        def _():
            all_back(c, c).wait_send()

        return carry

    lax.fori_loop(0, n, finish, 0)
    for g in range(2):
        all_back(n - 1, n - 1 + g, g).wait_send()
    for copy in metas:
        copy.wait_send()


PIECES = 4


def hand_over(*refs):
    results, outs, held, in_sem, out_sem = refs[:5], refs[5:10], refs[10:15], refs[15], refs[16]
    ins, backs = [], []
    for i in (2, 3, 4, 0, 1):
        rows = results[i].shape[-2] // PIECES
        for p in range(PIECES):
            at = (0,) * (len(results[i].shape) - 2) + (pl.ds(p * rows, rows),)
            ins.append(pltpu.make_async_copy(results[i].at[at], held[i].at[at], in_sem.at[i, p]))
            backs.append(pltpu.make_async_copy(held[i].at[at], outs[i].at[at], out_sem.at[i, p]))
    for copy in ins:
        copy.start()
    for copy, back in zip(ins, backs):
        copy.wait()
        back.start()
    for back in backs:
        back.wait()


def local(tokens, cotangent, expert_ids, gate_values, w_gate, w_up, w_down):
    tok_rows, width = tokens.shape
    hidden = w_gate.shape[1]
    n = width // WIDE
    rows = PLANE * SOURCE_ROWS
    half = PLANE * 16
    sem = pltpu.SemaphoreType.DMA
    vmem, hbm = pl.BlockSpec(memory_space=pltpu.VMEM), pl.BlockSpec(memory_space=pl.ANY)
    results = pl.pallas_call(
        kernel,
        out_shape=[jax.ShapeDtypeStruct(v.shape, BF16) for v in (tokens, cotangent, w_gate, w_up, w_down)],
        in_specs=[vmem] * 2 + [hbm] * 5,
        out_specs=[hbm] * 5,
        scratch_shapes=[
            pltpu.VMEM((n, RING, 2, tok_rows, WIDE), BF16),
            pltpu.VMEM((n, PLANE, 2, SOURCE_ROWS, WIDE), BF16),
            pltpu.VMEM((n, PLANE, 2, SOURCE_ROWS, WIDE), BF16),
            pltpu.VMEM((n, PLANE, 2, SOURCE_ROWS, WIDE), BF16),
            pltpu.VMEM((n, 2, 4, 2, tok_rows, WIDE), BF16),
            pltpu.VMEM((3, n, hidden, WIDE), BF16),
            pltpu.VMEM((rows, 3 * hidden), F32),
            pltpu.VMEM((3, 4, rows // 4, hidden), BF16),
            pltpu.VMEM((3, 4, hidden, rows // 4), BF16),
            pltpu.VMEM((2, half, 4 * tok_rows), BF16),
            pltpu.VMEM((3, 2, 4 * tok_rows, half), BF16),
            pltpu.VMEM((2, half, 128), F32),
            pltpu.VMEM((RING, 8, tok_rows), F32),
            sem((n, 2)), sem, sem((RING,)), sem((RING,)), sem((n, 8, 2)), sem((n, 8, 2)),
            sem((n,)), sem((n,)), sem((n + 1,)), sem((n + 1,)), sem((n, 2, 4, 2)), sem((n, 2, 4, 2)), sem((n, 2)), sem((n, 3)),
        ],
        compiler_params=pltpu.CompilerParams(
            collective_id=0, has_side_effects=True, vmem_limit_bytes=63 * 2**20
        ),
    )(expert_ids.T, gate_values.T, tokens, cotangent, w_gate, w_up, w_down)
    return pl.pallas_call(
        hand_over,
        out_shape=[jax.ShapeDtypeStruct(v.shape, v.dtype) for v in results],
        in_specs=[pl.BlockSpec(memory_space=pltpu.HBM)] * 5,
        out_specs=[pl.BlockSpec(memory_space=pltpu.HBM)] * 5,
        scratch_shapes=[pltpu.VMEM(v.shape, v.dtype) for v in results] + [sem((5, PIECES)), sem((5, PIECES))],
    )(*results)


def solution(mesh):
    rows = P(("zero", "expert"), None)
    weights = P("expert", "zero", None)
    return jax.shard_map(
        local,
        mesh=mesh,
        in_specs=(rows, rows, rows, rows, weights, weights, weights),
        out_specs=(rows, rows, weights, weights, weights),
        check_vma=False,
    )
```

```python
import functools

import jax
import jax.numpy as jnp
from jax import lax
from jax.experimental import pallas as pl
from jax.experimental.pallas import tpu as pltpu
from jax.sharding import PartitionSpec as P

MESH = pl.DeviceIdType.MESH
BF16, F32, I32 = jnp.bfloat16, jnp.float32, jnp.int32

RING = 8
PLANE = 32
WIDE = 256
CAP = 4
LAG = 3
SOURCE_ROWS = RING * CAP
FROM_LEFT = {0: 0, 1: 1, 2: 3, 3: 5, 4: 7}
FROM_RIGHT = {0: 0, 1: 2, 2: 4, 3: 6, 4: 7}


def dot(a, b):
    return lax.dot_general(a, b, (((1,), (0,)), ((), ())), preferred_element_type=F32)


def dot_nt(a, b):
    return lax.dot_general(a, b, (((1,), (1,)), ((), ())), preferred_element_type=F32)


def kernel(
    ids_r, gate_r, tok, cot, wg, wu, wd,
    layer_out, token_grad, grad_gate, grad_up, grad_down,
    G, S, X, Q, RS, WB, F, H, T, D, C, GR, M,
    load_sem, wload_sem, meta_send, meta_recv, ring_send, ring_recv,
    out_send, out_recv, back_send, back_recv, rs_send, rs_recv, store_sem, wstore_sem,
):
    n = G.shape[0]
    tok_rows = G.shape[3]
    expert = lax.axis_index("expert")
    core = expert % 2
    z_lo = (expert // 2) % 4
    x = (expert // 8) % 4
    y = expert // 32
    z = lax.axis_index("zero") * 4 + z_lo

    def along_z(step):
        to = (z + step + RING) % RING
        return (to // 4, ((y * 4 + x) * 4 + to % 4) * 2 + core)

    def in_plane(j, sign):
        to_y = (y + sign * (j // 8) + 4) % 4
        to_x = (x + sign * ((j // 2) % 4) + 4) % 4
        to_c = (core + j % 2) % 2
        return (z // 4, ((to_y * 4 + to_x) * 4 + z_lo) * 2 + to_c)

    def columns(c):
        return pl.ds(pl.multiple_of(c * WIDE, WIDE), WIDE)

    def loads(c):
        return [
            pltpu.make_async_copy(ref.at[:, columns(c)], G.at[c, 0, a], load_sem.at[c, a])
            for a, ref in enumerate((tok, cot))
        ]

    def start_load(c, carry):
        for copy in loads(c):
            copy.start()
        return carry

    start_load(0, 0)
    barrier = pltpu.get_barrier_semaphore()

    def greet(j, carry):
        pl.semaphore_signal(barrier, inc=1, device_id=in_plane(j, 1), device_id_type=MESH)
        return carry

    lax.fori_loop(1, PLANE, greet, 0)
    for step in range(1, RING):
        pl.semaphore_signal(barrier, inc=1, device_id=along_z(step), device_id_type=MESH)

    def start_weights(c, carry):
        for i, ref in enumerate((wg, wu, wd)):
            pltpu.make_async_copy(ref.at[0, :, columns(c)], WB.at[i, c], wload_sem).start()
        return carry

    earlier = lax.broadcasted_iota(I32, (tok_rows, tok_rows), 0) < lax.broadcasted_iota(
        I32, (tok_rows, tok_rows), 1
    )
    M[0] = jnp.zeros((8, tok_rows), F32)
    M[0, 0:2, :] = ids_r[...].astype(F32)
    ids_c = jnp.transpose(M[0])
    for k in range(2):
        own = ids_r[k : k + 1, :].astype(F32)
        same = jnp.zeros((tok_rows, tok_rows), F32)
        for k2 in range(2):
            same += jnp.where((ids_c[:, k2 : k2 + 1] == own) & earlier, 1.0, 0.0)
        slot = jnp.sum(same, axis=0, keepdims=True)
        M[0, k : k + 1, :] = own * CAP + slot
    M[0, 2:4, :] = gate_r[...]

    pl.semaphore_wait(barrier, PLANE - 1 + RING - 1)

    def remote(src, dst, send, recv, to):
        return pltpu.make_async_remote_copy(
            src_ref=src, dst_ref=dst, send_sem=send, recv_sem=recv, device_id=to, device_id_type=MESH
        )

    right, left = along_z(1), along_z(-1)

    def ring_copies(c, hop, a):
        got_l, got_r = FROM_LEFT[hop - 1], FROM_RIGHT[hop - 1]
        to_l, to_r = FROM_LEFT[hop], FROM_RIGHT[hop]
        ways = (
            (got_l, to_l, 2 * hop - 2, right),
            (got_r, to_r, 2 * hop - 1, left),
        )
        if hop == 4:
            ways = ways[a : a + 1]
        return [
            remote(G.at[c, got, a], G.at[c, to, a], ring_send.at[c, number, a], ring_recv.at[c, to, a], whom)
            for got, to, number, whom in ways
        ]

    def ring_hop(c, hop):
        for a in range(2):
            if hop == 1:
                loads(c)[a].wait()
            else:
                for copy in came_in(c, hop - 1, a, hop == 4):
                    copy.wait_recv()
            for copy in ring_copies(c, hop, a):
                copy.start()

    def came_in(c, hop, a, forwarded=False):
        copies = ring_copies(c, hop, a)
        return copies[a : a + 1] if forwarded else copies

    def ring_end(c):
        for a in range(2):
            ring_copies(c, 3, a)[1 - a].wait_recv()
        for a in range(2):
            ring_copies(c, 4, a)[0].wait_recv()

    ring_hop(0, 1)
    metas = []
    for slot, step in enumerate((0, 1, -1, 2, -2, 3, -3, 4)):
        if step:
            metas.append(remote(M.at[0], M.at[slot], meta_send.at[slot], meta_recv.at[slot], along_z(step)))
    for copy in metas:
        copy.start()
    lax.fori_loop(1, n, start_load, 0)
    ring_hop(0, 2)
    for copy in metas:
        copy.wait_recv()

    def place(position, i):
        e = position.astype(I32) // CAP
        s = position.astype(I32) % CAP
        mine = ((e // 2) % 4) == z_lo
        j = ((e // 32 - y + 4) % 4) * 8 + ((e // 8 - x + 4) % 4) * 2 + (e - core + 2) % 2
        return jnp.where(mine, j * 16 + i * CAP + s, -1)

    half = PLANE * 16

    def build_pick(g):
        row_id = lax.broadcasted_iota(I32, (half, tok_rows), 0)
        gates = jnp.zeros((half, tok_rows), F32)
        for i in range(4):
            m = M[4 * g + i]
            first, second = row_id == place(m[0:1], i), row_id == place(m[1:2], i)
            D[g, :, i * tok_rows : (i + 1) * tok_rows] = jnp.where(first | second, 1.0, 0.0).astype(BF16)
            gates += jnp.where(first, m[2:3], 0.0) + jnp.where(second, m[3:4], 0.0)
        GR[g] = jnp.broadcast_to(jnp.sum(gates, axis=1, keepdims=True), (half, 128))

    def build_put(g):
        col_id = lax.broadcasted_iota(I32, (tok_rows, half), 1)
        for i in range(4):
            mt = jnp.transpose(M[4 * g + i])
            tokens_i = slice(i * tok_rows, (i + 1) * tok_rows)
            first, second = col_id == place(mt[:, 0:1], i), col_id == place(mt[:, 1:2], i)
            C[0, g, tokens_i, :] = jnp.where(first | second, 1.0, 0.0).astype(BF16)
            weight = jnp.where(first, mt[:, 2:3], 0.0) + jnp.where(second, mt[:, 3:4], 0.0)
            high = weight.astype(BF16)
            C[1, g, tokens_i, :] = high
            C[2, g, tokens_i, :] = (weight - high.astype(F32)).astype(BF16)

    def group(g):
        return slice(16 * g, 16 * g + 16)

    def pick(c, g):
        for a in range(2):
            block = G[c, 4 * g : 4 * g + 4, a].reshape(4 * tok_rows, WIDE)
            picked = dot(D[g], block)
            if a == 1:
                picked = picked * jnp.concatenate([GR[g]] * (WIDE // 128), axis=1)
            S[c, :, a, group(g), :] = picked.astype(BF16).reshape(PLANE, 16, WIDE)
        X[c, 0, :, group(g), :] = S[c, 0, :, group(g), :]

    def send(c, dst, sign, send_sem, recv_sem, g=None):
        rows = slice(0, SOURCE_ROWS) if g is None else group(g)

        def one(k, carry):
            j = (k * 11) % PLANE
            remote(S.at[c, j, :, rows], dst.at[c, j, :, rows], send_sem, recv_sem, in_plane(j, sign)).start()
            return carry

        lax.fori_loop(1, PLANE, one, 0)

    def all_of(c, dst, send_sem, recv_sem, g=None):
        others, rows = pl.ds(1, PLANE - 1), slice(0, SOURCE_ROWS) if g is None else group(g)
        return remote(S.at[c, others, :, rows], dst.at[c, others, :, rows], send_sem, recv_sem, right)

    def all_out(c):
        return all_of(c, X, out_send.at[c], out_recv.at[c])

    def row_tile(c, a, m):
        return X[c, pl.ds(8 * m, 8), a].reshape(8 * SOURCE_ROWS, WIDE)

    def tile_rows(m):
        return pl.ds(pl.multiple_of(m * 256, 256), 256)

    def unit_cols(i):
        units = WB.shape[2]
        return slice(i * units, (i + 1) * units)

    def before_act(c):
        all_out(c).wait_recv()

        def tile(m, carry):
            rows, cots = row_tile(c, 0, m), row_tile(c, 1, m)
            for i, block in enumerate((rows, rows, cots)):
                F[tile_rows(m), unit_cols(i)] += dot_nt(block, WB[i, c])
            return carry

        lax.fori_loop(0, 4, tile, 0)

    def send_out(c, g=None):
        send(c, X, 1, out_send.at[c], out_recv.at[c], g)

    build_pick(0)
    ring_hop(0, 3)
    ring_hop(1, 1)
    pick(0, 0)
    send_out(0, 0)
    lax.fori_loop(0, n, start_weights, 0)
    build_pick(1)
    ring_hop(0, 4)
    ring_hop(1, 2)
    ring_hop(2, 1)
    F[...] = jnp.zeros(F.shape, F32)
    ring_end(0)
    pick(0, 1)
    send_out(0, 1)
    ring_hop(1, 3)
    ring_hop(2, 2)
    ring_hop(3, 1)
    ring_hop(1, 4)
    ring_hop(2, 3)
    ring_hop(3, 2)
    ring_hop(4, 1)
    pltpu.make_async_copy(WB, WB, wload_sem).wait()

    def way_out(t, carry):
        ring_end(t)
        pick(t, 0)
        pick(t, 1)
        send_out(t)
        for ahead in range(1, 5):

            @pl.when(t + ahead < n)
            def _(ahead=ahead):
                ring_hop(t + ahead, 5 - ahead)

        @pl.when(t >= 2)
        def _():
            before_act(t - 2)

        return carry

    lax.fori_loop(1, n, way_out, 0)
    build_put(0)
    build_put(1)
    before_act(n - 2)
    before_act(n - 1)

    def activate(m, carry):
        pre_gate, pre_up, hidden_grad = (F[tile_rows(m), unit_cols(i)] for i in range(3))
        sigmoid = jax.nn.sigmoid(pre_gate)
        silu = pre_gate * sigmoid
        hidden = silu * pre_up
        gate_grad = hidden_grad * pre_up * (sigmoid * (1.0 + pre_gate * (1.0 - sigmoid)))
        up_grad = hidden_grad * silu
        for i, v in enumerate((gate_grad, up_grad, hidden)):
            H[i, m] = v.astype(BF16)
            T[i, m] = jnp.transpose(v).astype(BF16)
        return carry

    lax.fori_loop(0, 4, activate, 0)

    def answer(c, carry):
        all_out(c).wait_send()

        def tile(m, carry):
            expert_out = dot(H[2, m], WB[2, c])
            row_grad = dot(H[0, m], WB[0, c]) + dot(H[1, m], WB[1, c])
            S[c, pl.ds(8 * m, 8), 0] = expert_out.astype(BF16).reshape(8, SOURCE_ROWS, WIDE)
            S[c, pl.ds(8 * m, 8), 1] = row_grad.astype(BF16).reshape(8, SOURCE_ROWS, WIDE)
            return carry

        lax.fori_loop(0, 4, tile, 0)
        Q[c, 0] = S[c, 0]

        @pl.when(c < n - 1)
        def _():
            send(c, Q, -1, back_send.at[c], back_recv.at[c])

        return carry

    lax.fori_loop(0, n, answer, 0)
    for g in (1, 0):
        send(n - 1, Q, -1, back_send.at[n - 1 + g], back_recv.at[n - 1 + g], g)

    def ring_sent(c, carry):
        for hop in range(1, 5):
            for a in range(2):
                for copy in ring_copies(c, hop, a):
                    copy.wait_send()
        return carry

    lax.fori_loop(0, n, ring_sent, 0)

    def part(c, slot, a):
        g, frames = slot // 4, slice((slot % 4) * tok_rows, (slot % 4 + 1) * tok_rows)
        rows = Q[c, :, a, group(g), :].reshape(half, WIDE)
        if a == 0:
            return dot(C[1, g, frames, :], rows) + dot(C[2, g, frames, :], rows)
        return dot(C[0, g, frames, :], rows)

    def rs_copies(c, hop, a):
        if hop == 1:
            return [remote(G.at[c, 7, a], RS.at[c, a, 3, a], rs_send.at[c, a, 3, a], rs_recv.at[c, a, 3, a], (right, left)[a])]
        at, to = 5 - hop, 4 - hop
        return [
            remote(RS.at[c, way, at, a], RS.at[c, way, to, a], rs_send.at[c, way, to, a], rs_recv.at[c, way, to, a], whom)
            for way, whom in enumerate((right, left))
        ]

    def rs_hop(c, hop, ways=(0, 1)):
        for a in range(2):
            copies = rs_copies(c, hop, a)
            if hop == 1:
                G[c, 7, a] = part(c, 7, a).astype(BF16)
                copies[0].start()
                continue
            at = 5 - hop
            for way in ways:
                total = part(c, (FROM_RIGHT, FROM_LEFT)[way][at], a)
                if hop > 2:
                    rs_copies(c, hop - 1, a)[way].wait_recv()
                elif a == way:
                    rs_copies(c, 1, a)[0].wait_recv()
                if hop > 2 or a == way:
                    total = total + RS[c, way, at, a].astype(F32)
                RS[c, way, at, a] = total.astype(BF16)
                copies[way].start()

    def stores(c):
        return [
            pltpu.make_async_copy(G.at[c, 0, a], ref.at[:, columns(c)], store_sem.at[c, a])
            for a, ref in enumerate((layer_out, token_grad))
        ]

    def rs_end(c):
        for a, copy in enumerate(stores(c)):
            total = part(c, 0, a)
            for way in range(2):
                rs_copies(c, 4, a)[way].wait_recv()
                total = total + RS[c, way, 0, a].astype(F32)
            G[c, 0, a] = total.astype(BF16)
            copy.start()

    def wstore(c, i):
        ref = (grad_gate, grad_up, grad_down)[i]
        return pltpu.make_async_copy(WB.at[i, c], ref.at[0, :, columns(c)], wstore_sem.at[c, i])

    def weight_grad(c, i):
        a = 1 if i == 2 else 0
        total = dot(T[i, 0], row_tile(c, a, 0))
        for m in range(1, 4):
            total += dot(T[i, m], row_tile(c, a, m))
        WB[i, c] = total.astype(BF16)
        wstore(c, i).start()

    def all_back(c, number, g=None):
        return all_of(c, Q, back_send.at[number], back_recv.at[number], g)

    def finish(c, carry):
        for copy in stores(c):
            copy.wait()
        for i in range(3):
            wstore(c, i).wait()
        for hop in range(1, 5):
            for a in range(2):
                for copy in rs_copies(c, hop, a):
                    copy.wait_send()

        @pl.when(c < n - 1)
        def _():
            all_back(c, c).wait_send()

        return carry

    def way_back(c, carry):
        all_back(c, c).wait_recv()
        rs_hop(c, 1)

        @pl.when(c >= 1)
        def _():
            rs_hop(c - 1, 3)

        @pl.when(c >= 2)
        def _():
            rs_end(c - 2)

        for i in range(3):
            weight_grad(c, i)
        rs_hop(c, 2)

        @pl.when(c >= 1)
        def _():
            rs_hop(c - 1, 4)

        @pl.when(c >= LAG)
        def _():
            finish(c - LAG, 0)

        return carry

    lax.fori_loop(0, n - 1, way_back, 0)
    all_back(n - 1, n, 1).wait_recv()
    rs_hop(n - 1, 1)
    rs_hop(n - 2, 3)
    rs_end(n - 3)
    rs_hop(n - 1, 2)
    rs_hop(n - 2, 4)
    rs_hop(n - 1, 3, (0,))
    all_back(n - 1, n - 1, 0).wait_recv()
    rs_hop(n - 1, 3, (1,))
    for i in range(3):
        weight_grad(n - 1, i)
    rs_end(n - 2)
    rs_hop(n - 1, 4)
    lax.fori_loop(n - LAG - 1, n - 1, finish, 0)
    rs_end(n - 1)
    finish(n - 1, 0)
    for g in range(2):
        all_back(n - 1, n - 1 + g, g).wait_send()
    for copy in metas:
        copy.wait_send()


PIECES = 4


def hand_over(*refs):
    results, outs, held, in_sem, out_sem = refs[:5], refs[5:10], refs[10:15], refs[15], refs[16]
    ins, backs = [], []
    for i in (2, 3, 4, 0, 1):
        rows = results[i].shape[-2] // PIECES
        for p in range(PIECES):
            at = (0,) * (len(results[i].shape) - 2) + (pl.ds(p * rows, rows),)
            ins.append(pltpu.make_async_copy(results[i].at[at], held[i].at[at], in_sem.at[i, p]))
            backs.append(pltpu.make_async_copy(held[i].at[at], outs[i].at[at], out_sem.at[i, p]))
    for copy in ins:
        copy.start()
    for copy, back in zip(ins, backs):
        copy.wait()
        back.start()
    for back in backs:
        back.wait()


def local(tokens, cotangent, expert_ids, gate_values, w_gate, w_up, w_down):
    tok_rows, width = tokens.shape
    hidden = w_gate.shape[1]
    n = width // WIDE
    rows = PLANE * SOURCE_ROWS
    half = PLANE * 16
    sem = pltpu.SemaphoreType.DMA
    vmem, hbm = pl.BlockSpec(memory_space=pltpu.VMEM), pl.BlockSpec(memory_space=pl.ANY)
    results = pl.pallas_call(
        kernel,
        out_shape=[jax.ShapeDtypeStruct(v.shape, BF16) for v in (tokens, cotangent, w_gate, w_up, w_down)],
        in_specs=[vmem] * 2 + [hbm] * 5,
        out_specs=[hbm] * 5,
        scratch_shapes=[
            pltpu.VMEM((n, RING, 2, tok_rows, WIDE), BF16),
            pltpu.VMEM((n, PLANE, 2, SOURCE_ROWS, WIDE), BF16),
            pltpu.VMEM((n, PLANE, 2, SOURCE_ROWS, WIDE), BF16),
            pltpu.VMEM((n, PLANE, 2, SOURCE_ROWS, WIDE), BF16),
            pltpu.VMEM((n, 2, 4, 2, tok_rows, WIDE), BF16),
            pltpu.VMEM((3, n, hidden, WIDE), BF16),
            pltpu.VMEM((rows, 3 * hidden), F32),
            pltpu.VMEM((3, 4, rows // 4, hidden), BF16),
            pltpu.VMEM((3, 4, hidden, rows // 4), BF16),
            pltpu.VMEM((2, half, 4 * tok_rows), BF16),
            pltpu.VMEM((3, 2, 4 * tok_rows, half), BF16),
            pltpu.VMEM((2, half, 128), F32),
            pltpu.VMEM((RING, 8, tok_rows), F32),
            sem((n, 2)), sem, sem((RING,)), sem((RING,)), sem((n, 8, 2)), sem((n, 8, 2)),
            sem((n,)), sem((n,)), sem((n + 1,)), sem((n + 1,)), sem((n, 2, 4, 2)), sem((n, 2, 4, 2)), sem((n, 2)), sem((n, 3)),
        ],
        compiler_params=pltpu.CompilerParams(
            collective_id=0, has_side_effects=True, vmem_limit_bytes=63 * 2**20
        ),
    )(expert_ids.T, gate_values.T, tokens, cotangent, w_gate, w_up, w_down)
    return pl.pallas_call(
        hand_over,
        out_shape=[jax.ShapeDtypeStruct(v.shape, v.dtype) for v in results],
        in_specs=[pl.BlockSpec(memory_space=pltpu.HBM)] * 5,
        out_specs=[pl.BlockSpec(memory_space=pltpu.HBM)] * 5,
        scratch_shapes=[pltpu.VMEM(v.shape, v.dtype) for v in results] + [sem((5, PIECES)), sem((5, PIECES))],
    )(*results)


def solution(mesh):
    rows = P(("zero", "expert"), None)
    weights = P("expert", "zero", None)
    return jax.shard_map(
        local,
        mesh=mesh,
        in_specs=(rows, rows, rows, rows, weights, weights, weights),
        out_specs=(rows, rows, weights, weights, weights),
        check_vma=False,
    )
```

```python
import functools

import jax
import jax.numpy as jnp
from jax import lax
from jax.experimental import pallas as pl
from jax.experimental.pallas import tpu as pltpu
from jax.sharding import PartitionSpec as P

MESH = pl.DeviceIdType.MESH
BF16, F32, I32 = jnp.bfloat16, jnp.float32, jnp.int32

RING = 8
PLANE = 32
WIDE = 256
CAP = 4
LAG = 3
SOURCE_ROWS = RING * CAP
FROM_LEFT = {0: 0, 1: 1, 2: 3, 3: 5, 4: 7}
FROM_RIGHT = {0: 0, 1: 2, 2: 4, 3: 6, 4: 7}


def dot(a, b):
    return lax.dot_general(a, b, (((1,), (0,)), ((), ())), preferred_element_type=F32)


def dot_nt(a, b):
    return lax.dot_general(a, b, (((1,), (1,)), ((), ())), preferred_element_type=F32)


def kernel(
    ids_r, gate_r, tok, cot, wg, wu, wd,
    layer_out, token_grad, grad_gate, grad_up, grad_down,
    G, S, X, Q, RS, WB, F, H, T, D, C, GR, M,
    load_sem, wload_sem, meta_send, meta_recv, ring_send, ring_recv,
    out_send, out_recv, back_send, back_recv, rs_send, rs_recv, store_sem, wstore_sem,
):
    n = G.shape[0]
    tok_rows = G.shape[3]
    expert = lax.axis_index("expert")
    core = expert % 2
    z_lo = (expert // 2) % 4
    x = (expert // 8) % 4
    y = expert // 32
    z = lax.axis_index("zero") * 4 + z_lo

    def along_z(step):
        to = (z + step + RING) % RING
        return (to // 4, ((y * 4 + x) * 4 + to % 4) * 2 + core)

    def in_plane(j, sign):
        to_y = (y + sign * (j // 8) + 4) % 4
        to_x = (x + sign * ((j // 2) % 4) + 4) % 4
        to_c = (core + j % 2) % 2
        return (z // 4, ((to_y * 4 + to_x) * 4 + z_lo) * 2 + to_c)

    def columns(c):
        return pl.ds(pl.multiple_of(c * WIDE, WIDE), WIDE)

    def loads(c):
        return [
            pltpu.make_async_copy(ref.at[:, columns(c)], G.at[c, 0, a], load_sem.at[c, a])
            for a, ref in enumerate((tok, cot))
        ]

    def start_load(c, carry):
        for copy in loads(c):
            copy.start()
        return carry

    start_load(0, 0)
    barrier = pltpu.get_barrier_semaphore()

    def greet(j, carry):
        pl.semaphore_signal(barrier, inc=1, device_id=in_plane(j, 1), device_id_type=MESH)
        return carry

    lax.fori_loop(1, PLANE, greet, 0)
    for step in range(1, RING):
        pl.semaphore_signal(barrier, inc=1, device_id=along_z(step), device_id_type=MESH)

    def start_weights(c, carry):
        for i, ref in enumerate((wg, wu, wd)):
            pltpu.make_async_copy(ref.at[0, :, columns(c)], WB.at[i, c], wload_sem).start()
        return carry

    earlier = lax.broadcasted_iota(I32, (tok_rows, tok_rows), 0) < lax.broadcasted_iota(
        I32, (tok_rows, tok_rows), 1
    )
    M[0] = jnp.zeros((8, tok_rows), F32)
    M[0, 0:2, :] = ids_r[...].astype(F32)
    ids_c = jnp.transpose(M[0])
    for k in range(2):
        own = ids_r[k : k + 1, :].astype(F32)
        same = jnp.zeros((tok_rows, tok_rows), F32)
        for k2 in range(2):
            same += jnp.where((ids_c[:, k2 : k2 + 1] == own) & earlier, 1.0, 0.0)
        slot = jnp.sum(same, axis=0, keepdims=True)
        M[0, k : k + 1, :] = own * CAP + slot
    M[0, 2:4, :] = gate_r[...]

    pl.semaphore_wait(barrier, PLANE - 1 + RING - 1)

    def remote(src, dst, send, recv, to):
        return pltpu.make_async_remote_copy(
            src_ref=src, dst_ref=dst, send_sem=send, recv_sem=recv, device_id=to, device_id_type=MESH
        )

    right, left = along_z(1), along_z(-1)

    def ring_copies(c, hop, a):
        got_l, got_r = FROM_LEFT[hop - 1], FROM_RIGHT[hop - 1]
        to_l, to_r = FROM_LEFT[hop], FROM_RIGHT[hop]
        ways = (
            (got_l, to_l, 2 * hop - 2, right),
            (got_r, to_r, 2 * hop - 1, left),
        )
        if hop == 4:
            ways = ways[a : a + 1]
        return [
            remote(G.at[c, got, a], G.at[c, to, a], ring_send.at[c, number, a], ring_recv.at[c, to, a], whom)
            for got, to, number, whom in ways
        ]

    def ring_hop(c, hop):
        for a in range(2):
            if hop == 1:
                loads(c)[a].wait()
            else:
                for copy in came_in(c, hop - 1, a, hop == 4):
                    copy.wait_recv()
            for copy in ring_copies(c, hop, a):
                copy.start()

    def came_in(c, hop, a, forwarded=False):
        copies = ring_copies(c, hop, a)
        return copies[a : a + 1] if forwarded else copies

    def ring_end(c):
        for a in range(2):
            ring_copies(c, 3, a)[1 - a].wait_recv()
        for a in range(2):
            ring_copies(c, 4, a)[0].wait_recv()

    ring_hop(0, 1)
    metas = []
    for slot, step in enumerate((0, 1, -1, 2, -2, 3, -3, 4)):
        if step:
            metas.append(remote(M.at[0], M.at[slot], meta_send.at[slot], meta_recv.at[slot], along_z(step)))
    for copy in metas:
        copy.start()
    lax.fori_loop(1, n, start_load, 0)
    ring_hop(0, 2)
    for copy in metas:
        copy.wait_recv()

    def place(position, i):
        e = position.astype(I32) // CAP
        s = position.astype(I32) % CAP
        mine = ((e // 2) % 4) == z_lo
        j = ((e // 32 - y + 4) % 4) * 8 + ((e // 8 - x + 4) % 4) * 2 + (e - core + 2) % 2
        return jnp.where(mine, j * 16 + i * CAP + s, -1)

    half = PLANE * 16

    def build_pick(g):
        row_id = lax.broadcasted_iota(I32, (half, tok_rows), 0)
        gates = jnp.zeros((half, tok_rows), F32)
        for i in range(4):
            m = M[4 * g + i]
            first, second = row_id == place(m[0:1], i), row_id == place(m[1:2], i)
            D[g, :, i * tok_rows : (i + 1) * tok_rows] = jnp.where(first | second, 1.0, 0.0).astype(BF16)
            gates += jnp.where(first, m[2:3], 0.0) + jnp.where(second, m[3:4], 0.0)
        GR[g] = jnp.broadcast_to(jnp.sum(gates, axis=1, keepdims=True), (half, 128))

    def build_put(g):
        col_id = lax.broadcasted_iota(I32, (tok_rows, half), 1)
        for i in range(4):
            mt = jnp.transpose(M[4 * g + i])
            tokens_i = slice(i * tok_rows, (i + 1) * tok_rows)
            first, second = col_id == place(mt[:, 0:1], i), col_id == place(mt[:, 1:2], i)
            C[0, g, tokens_i, :] = jnp.where(first | second, 1.0, 0.0).astype(BF16)
            weight = jnp.where(first, mt[:, 2:3], 0.0) + jnp.where(second, mt[:, 3:4], 0.0)
            high = weight.astype(BF16)
            C[1, g, tokens_i, :] = high
            C[2, g, tokens_i, :] = (weight - high.astype(F32)).astype(BF16)

    def group(g):
        return slice(16 * g, 16 * g + 16)

    def pick(c, g):
        for a in range(2):
            block = G[c, 4 * g : 4 * g + 4, a].reshape(4 * tok_rows, WIDE)
            picked = dot(D[g], block)
            if a == 1:
                picked = picked * jnp.concatenate([GR[g]] * (WIDE // 128), axis=1)
            S[c, :, a, group(g), :] = picked.astype(BF16).reshape(PLANE, 16, WIDE)
        X[c, 0, :, group(g), :] = S[c, 0, :, group(g), :]

    def send(c, dst, sign, send_sem, recv_sem, g=None):
        rows = slice(0, SOURCE_ROWS) if g is None else group(g)

        def one(k, carry):
            j = (k * 11) % PLANE
            remote(S.at[c, j, :, rows], dst.at[c, j, :, rows], send_sem, recv_sem, in_plane(j, sign)).start()
            return carry

        lax.fori_loop(1, PLANE, one, 0)

    def all_of(c, dst, send_sem, recv_sem, g=None):
        others, rows = pl.ds(1, PLANE - 1), slice(0, SOURCE_ROWS) if g is None else group(g)
        return remote(S.at[c, others, :, rows], dst.at[c, others, :, rows], send_sem, recv_sem, right)

    def all_out(c):
        return all_of(c, X, out_send.at[c], out_recv.at[c])

    def row_tile(c, a, m):
        return X[c, pl.ds(8 * m, 8), a].reshape(8 * SOURCE_ROWS, WIDE)

    def tile_rows(m):
        return pl.ds(pl.multiple_of(m * 256, 256), 256)

    def unit_cols(i):
        units = WB.shape[2]
        return slice(i * units, (i + 1) * units)

    def before_act(c):
        all_out(c).wait_recv()

        def tile(m, carry):
            rows, cots = row_tile(c, 0, m), row_tile(c, 1, m)
            for i, block in enumerate((rows, rows, cots)):
                F[tile_rows(m), unit_cols(i)] += dot_nt(block, WB[i, c])
            return carry

        lax.fori_loop(0, 4, tile, 0)

    def send_out(c, g=None):
        send(c, X, 1, out_send.at[c], out_recv.at[c], g)

    build_pick(0)
    ring_hop(0, 3)
    ring_hop(1, 1)
    pick(0, 0)
    send_out(0, 0)
    lax.fori_loop(0, n, start_weights, 0)
    build_pick(1)
    ring_hop(0, 4)
    ring_hop(1, 2)
    ring_hop(2, 1)
    F[...] = jnp.zeros(F.shape, F32)
    ring_end(0)
    pick(0, 1)
    send_out(0, 1)
    ring_hop(1, 3)
    ring_hop(2, 2)
    ring_hop(3, 1)
    ring_hop(1, 4)
    ring_hop(2, 3)
    ring_hop(3, 2)
    ring_hop(4, 1)
    pltpu.make_async_copy(WB, WB, wload_sem).wait()

    def way_out(t, carry):
        ring_end(t)
        pick(t, 0)
        pick(t, 1)
        send_out(t)
        for ahead in range(1, 5):

            @pl.when(t + ahead < n)
            def _(ahead=ahead):
                ring_hop(t + ahead, 5 - ahead)

        @pl.when(t >= 2)
        def _():
            before_act(t - 2)

        return carry

    lax.fori_loop(1, n, way_out, 0)
    build_put(0)
    build_put(1)
    before_act(n - 2)
    before_act(n - 1)

    def activate(m, carry):
        pre_gate, pre_up, hidden_grad = (F[tile_rows(m), unit_cols(i)] for i in range(3))
        sigmoid = jax.nn.sigmoid(pre_gate)
        silu = pre_gate * sigmoid
        hidden = silu * pre_up
        gate_grad = hidden_grad * pre_up * (sigmoid * (1.0 + pre_gate * (1.0 - sigmoid)))
        up_grad = hidden_grad * silu
        for i, v in enumerate((gate_grad, up_grad, hidden)):
            H[i, m] = v.astype(BF16)
            T[i, m] = jnp.transpose(v).astype(BF16)
        return carry

    lax.fori_loop(0, 4, activate, 0)

    def answer(c, carry):
        all_out(c).wait_send()

        def tile(m, carry):
            expert_out = dot(H[2, m], WB[2, c])
            row_grad = dot(H[0, m], WB[0, c]) + dot(H[1, m], WB[1, c])
            S[c, pl.ds(8 * m, 8), 0] = expert_out.astype(BF16).reshape(8, SOURCE_ROWS, WIDE)
            S[c, pl.ds(8 * m, 8), 1] = row_grad.astype(BF16).reshape(8, SOURCE_ROWS, WIDE)
            return carry

        lax.fori_loop(0, 4, tile, 0)
        Q[c, 0] = S[c, 0]

        @pl.when(c < n - 2)
        def _():
            send(c, Q, -1, back_send.at[c], back_recv.at[c])

        return carry

    lax.fori_loop(0, n, answer, 0)
    for g in (1, 0):
        for c in (n - 2, n - 1):
            send(c, Q, -1, back_send.at[c + 2 * g], back_recv.at[c + 2 * g], g)

    def ring_sent(c, carry):
        for hop in range(1, 5):
            for a in range(2):
                for copy in ring_copies(c, hop, a):
                    copy.wait_send()
        return carry

    lax.fori_loop(0, n, ring_sent, 0)

    def part(c, slot, a):
        g, frames = slot // 4, slice((slot % 4) * tok_rows, (slot % 4 + 1) * tok_rows)
        rows = Q[c, :, a, group(g), :].reshape(half, WIDE)
        if a == 0:
            return dot(C[1, g, frames, :], rows) + dot(C[2, g, frames, :], rows)
        return dot(C[0, g, frames, :], rows)

    def rs_copies(c, hop, a):
        if hop == 1:
            return [remote(G.at[c, 7, a], RS.at[c, a, 3, a], rs_send.at[c, a, 3, a], rs_recv.at[c, a, 3, a], (right, left)[a])]
        at, to = 5 - hop, 4 - hop
        return [
            remote(RS.at[c, way, at, a], RS.at[c, way, to, a], rs_send.at[c, way, to, a], rs_recv.at[c, way, to, a], whom)
            for way, whom in enumerate((right, left))
        ]

    def rs_hop(c, hop, ways=(0, 1)):
        for a in range(2):
            copies = rs_copies(c, hop, a)
            if hop == 1:
                G[c, 7, a] = part(c, 7, a).astype(BF16)
                copies[0].start()
                continue
            at = 5 - hop
            for way in ways:
                total = part(c, (FROM_RIGHT, FROM_LEFT)[way][at], a)
                if hop > 2:
                    rs_copies(c, hop - 1, a)[way].wait_recv()
                elif a == way:
                    rs_copies(c, 1, a)[0].wait_recv()
                if hop > 2 or a == way:
                    total = total + RS[c, way, at, a].astype(F32)
                RS[c, way, at, a] = total.astype(BF16)
                copies[way].start()

    def stores(c):
        return [
            pltpu.make_async_copy(G.at[c, 0, a], ref.at[:, columns(c)], store_sem.at[c, a])
            for a, ref in enumerate((layer_out, token_grad))
        ]

    def rs_end(c):
        for a, copy in enumerate(stores(c)):
            total = part(c, 0, a)
            for way in range(2):
                rs_copies(c, 4, a)[way].wait_recv()
                total = total + RS[c, way, 0, a].astype(F32)
            G[c, 0, a] = total.astype(BF16)
            copy.start()

    def wstore(c, i):
        ref = (grad_gate, grad_up, grad_down)[i]
        return pltpu.make_async_copy(WB.at[i, c], ref.at[0, :, columns(c)], wstore_sem.at[c, i])

    def weight_grad(c, i):
        a = 1 if i == 2 else 0
        total = dot(T[i, 0], row_tile(c, a, 0))
        for m in range(1, 4):
            total += dot(T[i, m], row_tile(c, a, m))
        WB[i, c] = total.astype(BF16)
        wstore(c, i).start()

    def all_back(c, number, g=None):
        return all_of(c, Q, back_send.at[number], back_recv.at[number], g)

    def finish(c, carry):
        for copy in stores(c):
            copy.wait()
        for i in range(3):
            wstore(c, i).wait()
        for hop in range(1, 5):
            for a in range(2):
                for copy in rs_copies(c, hop, a):
                    copy.wait_send()

        @pl.when(c < n - 2)
        def _():
            all_back(c, c).wait_send()

        return carry

    def way_back(c, carry):
        all_back(c, c).wait_recv()
        rs_hop(c, 1)

        @pl.when(c >= 1)
        def _():
            rs_hop(c - 1, 3)

        @pl.when(c >= 2)
        def _():
            rs_end(c - 2)

        for i in range(3):
            weight_grad(c, i)
        rs_hop(c, 2)

        @pl.when(c >= 1)
        def _():
            rs_hop(c - 1, 4)

        @pl.when(c >= LAG)
        def _():
            finish(c - LAG, 0)

        return carry

    def half_back(c, g):
        return all_back(c, c + 2 * g, g)

    lax.fori_loop(0, n - 2, way_back, 0)
    half_back(n - 2, 1).wait_recv()
    rs_hop(n - 2, 1)
    rs_hop(n - 3, 3)
    rs_end(n - 4)
    for i in range(3):
        weight_grad(n - 2, i)
    rs_hop(n - 2, 2)
    rs_hop(n - 3, 4)
    half_back(n - 1, 1).wait_recv()
    rs_hop(n - 1, 1)
    rs_hop(n - 2, 3, (0,))
    half_back(n - 2, 0).wait_recv()
    rs_hop(n - 2, 3, (1,))
    rs_end(n - 3)
    rs_hop(n - 1, 2)
    rs_hop(n - 2, 4)
    rs_hop(n - 1, 3, (0,))
    half_back(n - 1, 0).wait_recv()
    rs_hop(n - 1, 3, (1,))
    for i in range(3):
        weight_grad(n - 1, i)
    rs_end(n - 2)
    rs_hop(n - 1, 4)
    lax.fori_loop(n - LAG - 2, n - 1, finish, 0)
    rs_end(n - 1)
    finish(n - 1, 0)
    for c in (n - 2, n - 1):
        for g in range(2):
            half_back(c, g).wait_send()
    for copy in metas:
        copy.wait_send()


PIECES = 4


def hand_over(*refs):
    results, outs, held, in_sem, out_sem = refs[:5], refs[5:10], refs[10:15], refs[15], refs[16]
    ins, backs = [], []
    for i in (2, 3, 4, 0, 1):
        rows = results[i].shape[-2] // PIECES
        for p in range(PIECES):
            at = (0,) * (len(results[i].shape) - 2) + (pl.ds(p * rows, rows),)
            ins.append(pltpu.make_async_copy(results[i].at[at], held[i].at[at], in_sem.at[i, p]))
            backs.append(pltpu.make_async_copy(held[i].at[at], outs[i].at[at], out_sem.at[i, p]))
    for copy in ins:
        copy.start()
    for copy, back in zip(ins, backs):
        copy.wait()
        back.start()
    for back in backs:
        back.wait()


def local(tokens, cotangent, expert_ids, gate_values, w_gate, w_up, w_down):
    tok_rows, width = tokens.shape
    hidden = w_gate.shape[1]
    n = width // WIDE
    rows = PLANE * SOURCE_ROWS
    half = PLANE * 16
    sem = pltpu.SemaphoreType.DMA
    vmem, hbm = pl.BlockSpec(memory_space=pltpu.VMEM), pl.BlockSpec(memory_space=pl.ANY)
    results = pl.pallas_call(
        kernel,
        out_shape=[jax.ShapeDtypeStruct(v.shape, BF16) for v in (tokens, cotangent, w_gate, w_up, w_down)],
        in_specs=[vmem] * 2 + [hbm] * 5,
        out_specs=[hbm] * 5,
        scratch_shapes=[
            pltpu.VMEM((n, RING, 2, tok_rows, WIDE), BF16),
            pltpu.VMEM((n, PLANE, 2, SOURCE_ROWS, WIDE), BF16),
            pltpu.VMEM((n, PLANE, 2, SOURCE_ROWS, WIDE), BF16),
            pltpu.VMEM((n, PLANE, 2, SOURCE_ROWS, WIDE), BF16),
            pltpu.VMEM((n, 2, 4, 2, tok_rows, WIDE), BF16),
            pltpu.VMEM((3, n, hidden, WIDE), BF16),
            pltpu.VMEM((rows, 3 * hidden), F32),
            pltpu.VMEM((3, 4, rows // 4, hidden), BF16),
            pltpu.VMEM((3, 4, hidden, rows // 4), BF16),
            pltpu.VMEM((2, half, 4 * tok_rows), BF16),
            pltpu.VMEM((3, 2, 4 * tok_rows, half), BF16),
            pltpu.VMEM((2, half, 128), F32),
            pltpu.VMEM((RING, 8, tok_rows), F32),
            sem((n, 2)), sem, sem((RING,)), sem((RING,)), sem((n, 8, 2)), sem((n, 8, 2)),
            sem((n,)), sem((n,)), sem((n + 2,)), sem((n + 2,)), sem((n, 2, 4, 2)), sem((n, 2, 4, 2)), sem((n, 2)), sem((n, 3)),
        ],
        compiler_params=pltpu.CompilerParams(
            collective_id=0, has_side_effects=True, vmem_limit_bytes=63 * 2**20
        ),
    )(expert_ids.T, gate_values.T, tokens, cotangent, w_gate, w_up, w_down)
    return pl.pallas_call(
        hand_over,
        out_shape=[jax.ShapeDtypeStruct(v.shape, v.dtype) for v in results],
        in_specs=[pl.BlockSpec(memory_space=pltpu.HBM)] * 5,
        out_specs=[pl.BlockSpec(memory_space=pltpu.HBM)] * 5,
        scratch_shapes=[pltpu.VMEM(v.shape, v.dtype) for v in results] + [sem((5, PIECES)), sem((5, PIECES))],
    )(*results)


def solution(mesh):
    rows = P(("zero", "expert"), None)
    weights = P("expert", "zero", None)
    return jax.shard_map(
        local,
        mesh=mesh,
        in_specs=(rows, rows, rows, rows, weights, weights, weights),
        out_specs=(rows, rows, weights, weights, weights),
        check_vma=False,
    )
```
